256 devices in a mesh: tm: 32 (over y, x, core), slab: 8 (over z).
Axes of the slice: x: 4, y: 4, z: 8, core: 2. Of those that a mesh axis runs over, the one named last changes fastest.
Arguments:
- precision_blocks: bfloat16 [64, 1024, 1024], P('tm', None, 'slab'), may hold values from -0.2 to 0.2, as said below
- coupling: bfloat16 [64, 1024, 1024], P('tm'), may hold values from -0.03125 to 1.03125
Outputs:
- variance_blocks: bfloat16 [64, 1024, 1024], P('tm', None, 'slab')
The draws below stay inside these ranges and needn't reach their ends.
Inputs may be any that keep to these rules, and one draw needn't show every extreme that they name: `precision_blocks`: each block is symmetric positive definite.
All inputs are finite; a program needn't handle non-finite values.
Results may differ from the reference program's by a relative error of at most 0.0065.
The reference program's roundings to bfloat16 on the way count: a program that leaves them out, or rounds other values in their place, can miss the bound.
Values may be sent and summed in bfloat16 or wider, within the bound.
No kernel may reach another device: no remote copies, remote signals or barrier semaphores. Data moves between devices by JAX's collectives and lax.ppermute only.
A program may use at most 64 MiB of HBM per device.

```python
import math
import jax
import jax.numpy as jnp

B = 1024
BLK_DEV = 2
TOTAL_STEPS = 64
LEVELS = 5
N_TM = 32


def draw_precision_blocks(key, part):
    key = jax.random.fold_in(key, 7)
    random_keys = jax.random.split(key, 5)
    scales = jnp.exp(jax.random.uniform(random_keys[0], (TOTAL_STEPS, B), jnp.float32, math.log(0.1), math.log(0.35)))
    raw = jax.random.truncated_normal(random_keys[1], -4.0, 4.0, (TOTAL_STEPS, B, B), jnp.float32)
    sym = (raw + jnp.swapaxes(raw, 1, 2)) * (0.2 / math.sqrt(2.0 * B))
    order = jax.random.permutation(random_keys[2], B).astype(jnp.int32)
    place = jnp.argsort(order).astype(jnp.int32)
    partner = order[jnp.bitwise_xor(place, 1)]
    strength = jax.random.uniform(random_keys[3], (B // 2,), jnp.float32, 0.25, 0.45)
    flip = jax.random.uniform(random_keys[4], (B // 2,), jnp.float32)
    signed = jnp.where(flip < 0.5, -strength, strength)
    coefficient = signed[place // 2]
    columns = jnp.arange(B, dtype=jnp.int32)
    pair_matrix = jnp.where(columns[None, :] == partner[:, None], coefficient[:, None], 0.0)
    central_part = jnp.eye(B, dtype=jnp.float32)[None, :, :] + sym + pair_matrix[None, :, :]
    return (scales[:, :, None] * central_part * scales[:, None, :]).astype(jnp.bfloat16)


def draw_coupling(key, part):
    key = jax.random.fold_in(key, 11)
    random_keys = jax.random.split(key, 7)
    pick = jax.random.uniform(random_keys[0], (B,), jnp.float32)
    slow_rate = jax.random.uniform(random_keys[1], (B,), jnp.float32, 0.985, 0.999)
    brief_rate = jax.random.uniform(random_keys[2], (B,), jnp.float32, 0.93, 0.97)
    base_matrix = jnp.where(pick < 0.5, slow_rate, brief_rate)
    diagonal_nudge = jax.random.uniform(random_keys[3], (TOTAL_STEPS, 1, B), jnp.float32, 0.96, 1.0)
    spike_selector = jax.random.uniform(random_keys[4], (TOTAL_STEPS, 1, 1), jnp.float32)
    spike_magnitude = jax.random.uniform(random_keys[5], (TOTAL_STEPS, 1, 1), jnp.float32, 0.5, 0.8)
    spike_draw = jnp.where(spike_selector < 0.06, spike_magnitude, 1.0)
    noise = jax.random.truncated_normal(random_keys[6], -4.0, 4.0, (TOTAL_STEPS, B, B), jnp.float32) * (0.25 / math.sqrt(B))
    central_part = jnp.eye(B, dtype=jnp.float32)[None, :, :] + noise
    return (central_part * (base_matrix[None, None, :] * diagonal_nudge * spike_draw)).astype(jnp.bfloat16)


def setup_inputs(seed: int = 0) -> dict:
    key_list = jax.random.split(jax.random.key(seed), 3)
    precision_blocks = draw_precision_blocks(jax.random.fold_in(key_list[2], 71), 0)
    coupling = draw_coupling(jax.random.fold_in(key_list[2], 71), 0)
    return dict(precision_blocks=precision_blocks, coupling=coupling)


def product(left, right):
    return jnp.einsum("pij,pjk->pik", left.astype(jnp.float32), right.astype(jnp.float32))


def product_transposed(left, right):
    return jnp.einsum("pji,pjk->pik", left.astype(jnp.float32), right.astype(jnp.float32))


def later(blocks, distance):
    return jnp.concatenate([blocks[distance:], jnp.zeros_like(blocks[:distance])], axis=0)


def reference(precision_blocks, coupling):
    grouped_p = precision_blocks.reshape(N_TM, BLK_DEV, B, B)
    grouped_k = coupling.reshape(N_TM, BLK_DEV, B, B)
    first_p = grouped_p[:, 0]
    second_p = grouped_p[:, 1]
    first_k = grouped_k[:, 0]
    second_k = grouped_k[:, 1]
    mixed = product(second_p, first_k).astype(jnp.bfloat16)
    reduced = (first_p.astype(jnp.float32) + product_transposed(first_k, mixed)).astype(jnp.bfloat16)
    carried = product(second_k, first_k).astype(jnp.bfloat16)
    for depth_index in range(LEVELS):
        distance = 2 ** depth_index
        far_reduced = later(reduced, distance)
        far_carried = later(carried, distance)
        bridge = product(far_reduced, carried).astype(jnp.bfloat16)
        new_reduced = (reduced.astype(jnp.float32) + product_transposed(carried, bridge)).astype(jnp.bfloat16)
        if depth_index + 1 < LEVELS:
            carried = product(far_carried, carried).astype(jnp.bfloat16)
        reduced = new_reduced
    next_reduced = later(reduced, 1)
    weighed = product(next_reduced, second_k).astype(jnp.bfloat16)
    second_sigma = (second_p.astype(jnp.float32) + product_transposed(second_k, weighed)).astype(jnp.bfloat16)
    return jnp.stack([reduced, second_sigma], axis=1).reshape(TOTAL_STEPS, B, B)
```

```python
import jax
import jax.numpy as jnp
from jax import lax
from jax.sharding import Mesh, PartitionSpec as P

BF16 = jnp.bfloat16
F32 = jnp.float32
CHIPS = ("y", "x")


def dot(left, right):
    return jnp.dot(left, right, preferred_element_type=F32)


def from_later(block, distance):
    chips = lax.axis_size(CHIPS)
    return lax.ppermute(block, CHIPS, [(i + distance, i) for i in range(chips - distance)])


def from_other_core(block):
    return lax.ppermute(block, "core", [(0, 1), (1, 0)])


def turned(rows):
    slabs = lax.axis_size("z")
    m, n = rows.shape
    width = n // slabs
    pieces = rows.reshape(m, slabs, width).swapaxes(0, 1)
    return lax.all_to_all(pieces, "z", 0, 0, tiled=True)


def shards(precision_blocks, coupling):
    core = lax.axis_index("core")
    slab = lax.axis_index("z")
    width = precision_blocks.shape[2]
    half = width // 2
    order = precision_blocks.shape[1]
    first_k, second_k = coupling[0], coupling[1]
    rows = precision_blocks.swapaxes(1, 2)
    first_p, second_p = rows[0], rows[1]

    def side(a, b):
        return jnp.where(core == 0, a, b)

    own = dot(second_k, first_k).astype(BF16)
    other = from_other_core(own)
    c_low, c_high = side(own, other), side(other, own)
    whole = dot(c_high, c_low).astype(BF16)
    phi_last = side(dot(c_high, second_k).astype(BF16), second_k)

    def own_rows(full):
        return lax.dynamic_slice_in_dim(full, slab * width + core * half, half, 0)

    pieces = {1: own_rows(whole)}
    spans = {1: whole}
    levels = lax.axis_size(CHIPS).bit_length() - 1
    piece = pieces[1]
    for count in range(2, (1 << (levels - 1)) + 1):
        piece = dot(from_later(piece, 1), whole).astype(BF16)
        if count & (count - 1) == 0:
            spans[count] = lax.all_gather(piece, ("z", "core"), axis=0, tiled=True)

    z = dot(second_p, first_k).astype(BF16)
    cols = turned(z).reshape(order, width)
    part = (first_p.astype(F32) + dot(cols.T, first_k)).astype(BF16)

    def half_rows(block, which):
        return lax.dynamic_slice_in_dim(block, which * half, half, 0)

    def folded(base, x, c):
        z = dot(x, c).astype(BF16)
        got = turned(z)
        far = from_other_core(got)
        full = jnp.stack([side(got, far), side(far, got)], axis=1).reshape(order, width)
        y = half_rows(full.T, core)
        return (base.astype(F32) + dot(y, c)).astype(BF16)

    sent = half_rows(part, 1 - core)
    came = from_other_core(sent)
    kept = half_rows(part, core)
    reduced = folded(side(kept, came), side(came, kept), c_low)
    for level in range(levels):
        distance = 1 << level
        reduced = folded(reduced, from_later(reduced, distance), spans[distance])

    far = from_other_core(reduced)
    start = jnp.concatenate([side(reduced, far), side(far, reduced)], axis=0)
    after = from_later(reduced, 1)
    far_after = from_other_core(after)
    after = jnp.concatenate([side(after, far_after), side(far_after, after)], axis=0)
    part_high = from_other_core(part)
    left_a = side(part_high, after)
    right_a = side(second_k, own)
    z = jnp.concatenate([dot(left_a, right_a), dot(after, phi_last)], axis=0).astype(BF16)
    got = turned(z).reshape(8, 2, width, width)
    ya = got[:, 0].reshape(order, width).T
    yb = got[:, 1].reshape(order, width).T
    ta, tb = dot(ya, right_a), dot(yb, phi_last)
    out_a = side(start, (part.astype(F32) + ta).astype(BF16))
    out_b = (second_p.astype(F32) + side(ta + tb, tb)).astype(BF16)
    return jnp.stack([out_a, out_b], axis=0).swapaxes(1, 2)


def solution(mesh):
    grid = Mesh(mesh.devices.reshape(4, 4, 2, 8), ("y", "x", "core", "z"))
    return jax.shard_map(
        shards,
        mesh=grid,
        in_specs=(P(("y", "x", "core"), None, "z"), P(("y", "x", "core"), None, None)),
        out_specs=P(("y", "x", "core"), None, "z"),
        check_vma=False,
    )
```

```python
import jax
import jax.numpy as jnp
from jax import lax
from jax.sharding import Mesh, PartitionSpec as P

BF16 = jnp.bfloat16
F32 = jnp.float32
CHIPS = ("y", "x")


def dot(left, right):
    return jnp.dot(left, right, preferred_element_type=F32)


def tie(value, *others):
    return lax.optimization_barrier((value, *others))[0]


def moved(block, pairs):
    return lax.ppermute(block, CHIPS, pairs)


def from_other_core(block):
    return lax.ppermute(block, "core", [(0, 1), (1, 0)])


def turned(rows):
    slabs = lax.axis_size("z")
    m, n = rows.shape
    rows = lax.optimization_barrier(rows)
    pieces = rows.reshape(m, slabs, n // slabs).swapaxes(0, 1)
    return lax.all_to_all(pieces, "z", 0, 0, tiled=True)


def shards(precision_blocks, coupling):
    core = lax.axis_index("core")
    slab = lax.axis_index("z")
    chip = lax.axis_index(CHIPS)
    chips = lax.axis_size(CHIPS)
    order, width = precision_blocks.shape[1:]
    half = width // 2

    def side(a, b):
        return jnp.where(core == 0, a, b)

    def half_rows(block, which):
        return lax.dynamic_slice_in_dim(block, which * half, half, 0)

    def both_halves(block):
        far = from_other_core(block)
        return side(jnp.concatenate([block, far], axis=0), jnp.concatenate([far, block], axis=0))

    def later(distance):
        return [(i + distance, i) for i in range(chips - distance)]

    first_k, second_k = coupling[0], coupling[1]
    p_high = lax.ppermute(precision_blocks[0], "core", [(1, 0)])
    own = dot(second_k, first_k).astype(BF16)
    other = from_other_core(own)
    z_a = lax.dot_general(
        precision_blocks[1], first_k, (((0,), (0,)), ((), ())), preferred_element_type=F32
    ).astype(BF16)
    z_b = side(dot(p_high.T, own), dot(z_a, other)).astype(BF16)

    whole = dot(side(other, own), side(own, other)).astype(BF16)
    piece = lax.dynamic_slice_in_dim(whole, slab * width + core * half, half, 0)
    z_b, piece = lax.optimization_barrier((z_b, piece))
    got = turned(jnp.concatenate([z_a, z_b], axis=0))
    hop = moved(piece, later(1))
    mine = lax.dynamic_slice_in_dim(whole, core * (order // 2), order // 2, 1)
    near = moved(mine, [(i, i + 1) for i in range(chips - 1)])
    piece = dot(hop, whole).astype(BF16)
    piece = dot(moved(piece, later(1)), whole).astype(BF16)

    got, piece = lax.optimization_barrier((got, piece))
    hop = moved(piece, later(1))
    rows = precision_blocks.swapaxes(1, 2)
    first_p, second_p = rows[0].astype(F32), rows[1].astype(F32)
    got = got.reshape(8, 2, width, width)
    y_a = got[:, 0].reshape(order, width).T
    y_b = got[:, 1].reshape(order, width).T
    base = first_p + dot(y_a, first_k)
    part = base.astype(BF16)
    left = side(y_b, dot(y_b, first_k).astype(BF16))
    total = side(base + dot(left, own), dot(left, other))
    came = from_other_core(half_rows(total, 1 - core))
    reduced = (half_rows(total, core) + came).astype(BF16)

    def closed(base, got, times):
        far = from_other_core(got)
        full = jnp.stack([side(got, far), side(far, got)], axis=1).reshape(order, width)
        y = half_rows(full.T, core)
        return (base.astype(F32) + times(y)).astype(BF16)

    times = lambda x: dot(x, whole)
    x = moved(reduced, later(1))
    piece = dot(hop, whole).astype(BF16)
    near_piece = moved(piece, [(e, (e - 1) % chips) for e in range(chips)])
    far_piece = moved(piece, [(e + 4, (e - 1) % chips) for e in range(chips - 4)])
    near_piece, far_piece, near, x = lax.optimization_barrier((near_piece, far_piece, near, x))
    z = times(x).astype(BF16)
    both = lax.all_gather(
        jnp.stack([near_piece, far_piece], axis=0), ("z", "core"), axis=1, tiled=True
    )
    phi2_mine = dot(whole, near).astype(BF16)
    phi2_other = from_other_core(phi2_mine)
    got, phi2_mine = lax.optimization_barrier((turned(z), phi2_mine))
    reduced = closed(reduced, got, times)

    def times(x):
        mine, far = dot(x, phi2_mine), dot(x, phi2_other)
        return side(jnp.concatenate([mine, far], axis=1), jnp.concatenate([far, mine], axis=1))

    x = moved(reduced, [(c + 1, c) for c in range(1, chips - 1)])
    base = moved(reduced, [(c, (c + 1) % chips) for c in range(chips)])
    x, base = lax.optimization_barrier((x, base))
    reduced = closed(base, turned(times(x).astype(BF16)), times)

    x = moved(reduced, [((e + 5) % chips, (e - 1) % chips) for e in range(chips - 4)])
    base = moved(reduced, [((e + 1) % chips, (e - 1) % chips) for e in range(chips)])
    phi4, phi4_far = lax.optimization_barrier((both[0], both[1]))
    times = lambda x: dot(x, phi4)
    z = times(x).astype(BF16)
    phi8 = dot(tie(phi4_far, z), phi4).astype(BF16)
    got, base, phi8 = lax.optimization_barrier((turned(z), base, phi8))
    reduced = closed(base, got, times)
    times = lambda x: dot(x, phi8)
    x = moved(reduced, [((e + 7) % chips, (e - 1) % chips) for e in range(chips - 8)])
    reduced = closed(reduced, turned(times(x).astype(BF16)), times)

    start = moved(reduced, [(c, (c + 1) % chips) for c in range(chips)])
    after = jnp.where(chip == chips - 1, jnp.zeros_like(reduced), reduced)
    after = both_halves(after)
    part_high = lax.ppermute(part, "core", [(1, 0)])
    through = side(dot(after, other), dot(after, own)).astype(BF16)
    v = dot(side(part_high, after), second_k).astype(BF16)
    w = dot(through, second_k).astype(BF16)
    got = turned(jnp.concatenate([side(v, through), side(w, v)], axis=0))
    got = got.reshape(8, 2, width, width)
    y_a = got[:, 0].reshape(order, width).T
    y_b = got[:, 1].reshape(order, width).T
    w = side(dot(y_b, other), dot(y_a, own))
    q = side((y_a.astype(F32) + w).astype(BF16), y_b)
    out_b = (second_p + dot(q, second_k)).astype(BF16)
    out_a = side(both_halves(start), (part.astype(F32) + w).astype(BF16))
    return jnp.stack([out_a, out_b], axis=0).swapaxes(1, 2)


def solution(mesh):
    grid = Mesh(mesh.devices.reshape(4, 4, 2, 8), ("y", "x", "core", "z"))
    return jax.shard_map(
        shards,
        mesh=grid,
        in_specs=(P(("y", "x", "core"), None, "z"), P(("y", "x", "core"), None, None)),
        out_specs=P(("y", "x", "core"), None, "z"),
        check_vma=False,
    )
```

```python
import jax
import jax.numpy as jnp
from jax import lax
from jax.experimental import pallas as pl
from jax.experimental.pallas import tpu as pltpu
from jax.sharding import Mesh, PartitionSpec as P

BF16 = jnp.bfloat16
F32 = jnp.float32
CHIPS = ("y", "x")
VMEM = 60 * 2**20


def dot(left, right):
    return jnp.dot(left, right, preferred_element_type=F32)


def moved(block, pairs):
    return lax.ppermute(block, CHIPS, pairs)


def from_other_core(block):
    return lax.ppermute(block, "core", [(0, 1), (1, 0)])


def turned(rows):
    slabs = lax.axis_size("z")
    m, n = rows.shape
    rows = lax.optimization_barrier(rows)
    pieces = rows.reshape(m, slabs, n // slabs).swapaxes(0, 1)
    return lax.all_to_all(pieces, "z", 0, 0, tiled=True)


def fetch(source, target, sem, pieces=8):
    rows = target.shape[0] // pieces
    for i in range(pieces):
        part = pl.ds(i * rows, rows)
        pltpu.make_async_copy(source.at[part], target.at[part], sem).start()


def chip_close(core, got, first_p, coupling, own, other):
    _, order, width = first_p.shape
    slabs = order // width

    def kernel(core_ref, got_ref, p_ref, k_ref, own_ref, other_ref, part_ref, kept_ref,
               sent_ref, k, low, k_sem, low_sem):
        fetch(k_ref.at[0], k, k_sem)

        @pl.when(core_ref[0] == 0)
        def _():
            fetch(own_ref, low, low_sem)

        @pl.when(core_ref[0] == 1)
        def _():
            fetch(other_ref, low, low_sem)

        y_a = got_ref[:, 0].reshape(order, width).T
        y_b = got_ref[:, 1].reshape(order, width).T
        p = p_ref[0].T.astype(F32)
        pltpu.make_async_copy(k_ref.at[0], k, k_sem).wait()
        both = jnp.dot(
            jnp.concatenate([y_a, y_b], axis=0), k[...], preferred_element_type=F32
        )
        base = p + both[:width]
        part_ref[...] = base.astype(BF16)
        low_core = core_ref[0] == 0
        left = jnp.where(low_core, y_b.astype(F32), both[width:]).astype(BF16)
        pltpu.make_async_copy(own_ref, low, low_sem).wait()
        total = jnp.where(low_core, base, 0.0) + jnp.dot(
            left, low[...], preferred_element_type=F32
        )
        top, bottom = total[: width // 2], total[width // 2 :]
        kept_ref[...] = jnp.where(low_core, top, bottom)
        sent_ref[...] = jnp.where(low_core, bottom, top)

    whole = pl.BlockSpec(memory_space=pltpu.VMEM)
    hbm = pl.BlockSpec(memory_space=pl.ANY)
    return pl.pallas_call(
        kernel,
        in_specs=[pl.BlockSpec(memory_space=pltpu.SMEM), whole, whole, hbm, hbm, hbm],
        out_specs=[whole, whole, whole],
        out_shape=[
            jax.ShapeDtypeStruct((width, order), BF16),
            jax.ShapeDtypeStruct((width // 2, order), F32),
            jax.ShapeDtypeStruct((width // 2, order), F32),
        ],
        scratch_shapes=[
            pltpu.VMEM((order, order), BF16),
            pltpu.VMEM((order, order), BF16),
            pltpu.SemaphoreType.DMA,
            pltpu.SemaphoreType.DMA,
        ],
        cost_estimate=pl.CostEstimate(
            flops=width * order**2 // 8, bytes_accessed=order * order // 8, transcendentals=0
        ),
        compiler_params=pltpu.CompilerParams(vmem_limit_bytes=VMEM),
    )(core.reshape(1), got, first_p, coupling, own, other)


def last_close(core, got, start, part, precision_blocks, coupling, own, other):
    _, order, width = precision_blocks.shape

    def kernel(core_ref, got_ref, start_ref, part_ref, p_ref, k_ref, own_ref, other_ref, out_ref,
               k, high, k_sem, high_sem):
        low_core = core_ref[0] == 0

        @pl.when(low_core)
        def _():
            fetch(other_ref, high, high_sem)

        @pl.when(jnp.logical_not(low_core))
        def _():
            fetch(own_ref, high, high_sem)

        fetch(k_ref.at[1], k, k_sem)
        y_a = got_ref[:, 0].reshape(order, width).T
        y_b = got_ref[:, 1].reshape(order, width).T
        left = jnp.where(low_core, y_b.astype(F32), y_a.astype(F32)).astype(BF16)
        pltpu.make_async_copy(own_ref, high, high_sem).wait()
        w = jnp.dot(left, high[...], preferred_element_type=F32)
        q = jnp.where(low_core, y_a.astype(F32) + w, y_b.astype(F32)).astype(BF16)
        pltpu.make_async_copy(k_ref.at[1], k, k_sem).wait()
        second = jnp.dot(q, k[...], preferred_element_type=F32)
        out_ref[1] = (p_ref[0].astype(F32) + second.T).astype(BF16)
        first = jnp.where(low_core, start_ref[...].astype(F32), part_ref[...].astype(F32) + w)
        out_ref[0] = first.astype(BF16).T

    whole = pl.BlockSpec(memory_space=pltpu.VMEM)
    hbm = pl.BlockSpec(memory_space=pl.ANY)
    return pl.pallas_call(
        kernel,
        grid=(1,),
        in_specs=[
            pl.BlockSpec(memory_space=pltpu.SMEM),
            whole,
            whole,
            whole,
            pl.BlockSpec((1, order, width), lambda i: (1, 0, 0)),
            hbm,
            hbm,
            hbm,
        ],
        out_specs=pl.BlockSpec((2, order, width), lambda i: (0, 0, 0)),
        out_shape=jax.ShapeDtypeStruct((2, order, width), BF16),
        scratch_shapes=[
            pltpu.VMEM((order, order), BF16),
            pltpu.VMEM((order, order), BF16),
            pltpu.SemaphoreType.DMA,
            pltpu.SemaphoreType.DMA,
        ],
        cost_estimate=pl.CostEstimate(
            flops=4 * width * order**2, bytes_accessed=5 * order * order, transcendentals=0
        ),
        compiler_params=pltpu.CompilerParams(vmem_limit_bytes=VMEM),
    )(core.reshape(1), got, start, part, precision_blocks, coupling, own, other)


def shards(precision_blocks, coupling):
    core = lax.axis_index("core")
    slab = lax.axis_index("z")
    chip = lax.axis_index(CHIPS)
    chips = lax.axis_size(CHIPS)
    order, width = precision_blocks.shape[1:]
    half = width // 2

    def side(a, b):
        return jnp.where(core == 0, a, b)

    def half_rows(block, which):
        return lax.dynamic_slice_in_dim(block, which * half, half, 0)

    def both_halves(block):
        far = from_other_core(block)
        return side(jnp.concatenate([block, far], axis=0), jnp.concatenate([far, block], axis=0))

    def later(distance):
        return [(i + distance, i) for i in range(chips - distance)]

    def ahead_by(distance):
        return [((e + distance), (e - 1) % chips) for e in range(chips - distance)]

    p_high = lax.ppermute(precision_blocks[0], "core", [(1, 0)])
    own = dot(coupling[1], coupling[0]).astype(BF16)
    other = from_other_core(own)
    z_a = lax.dot_general(
        precision_blocks[1], coupling[0], (((0,), (0,)), ((), ())), preferred_element_type=F32
    ).astype(BF16)
    z_b = side(dot(p_high.T, own), dot(z_a, other)).astype(BF16)

    whole = dot(side(other, own), side(own, other)).astype(BF16)
    piece = lax.dynamic_slice_in_dim(whole, slab * width + core * half, half, 0)
    z_b, piece = lax.optimization_barrier((z_b, piece))
    got = turned(jnp.concatenate([z_a, z_b], axis=0))
    piece = dot(moved(piece, later(1)), whole).astype(BF16)
    got, piece = lax.optimization_barrier((got, piece))
    phi2 = lax.all_gather(piece, ("z", "core"), axis=0, tiled=True)
    hop = moved(piece, later(1))

    part, kept, sent = chip_close(
        core, got.reshape(8, 2, width, width), precision_blocks[:1], coupling, own, other
    )
    hop, kept = lax.optimization_barrier((hop, kept))
    piece = dot(hop, whole).astype(BF16)
    piece = dot(moved(piece, later(1)), whole).astype(BF16)
    pieces = [moved(piece, ahead_by(d)) for d in (0, 4, 8)]
    reduced = (kept + from_other_core(sent)).astype(BF16)

    def closed(base, got, times):
        far = from_other_core(got)
        full = jnp.stack([side(got, far), side(far, got)], axis=1).reshape(order, width)
        y = half_rows(full.T, core)
        return (base.astype(F32) + times(y)).astype(BF16)

    times = lambda x: dot(x, whole)
    x = moved(reduced, later(1))
    x, pieces = lax.optimization_barrier((x, pieces))
    gathered = lax.all_gather(jnp.stack(pieces), ("z", "core"), axis=1, tiled=True)
    reduced = closed(reduced, turned(times(x).astype(BF16)), times)
    times = lambda x: dot(x, phi2)
    x = moved(reduced, later(2))
    reduced = closed(reduced, turned(times(x).astype(BF16)), times)

    x1, x2, x3 = (moved(reduced, ahead_by(d)) for d in (4, 8, 12))
    base = moved(reduced, ahead_by(0))
    phis = lax.optimization_barrier((gathered[0], gathered[1], gathered[2]))
    z = dot(x3, phis[2]).astype(BF16)
    z = dot(jnp.concatenate([x2, z], axis=0), phis[1]).astype(BF16)
    z = dot(jnp.concatenate([x1, z], axis=0), phis[0]).astype(BF16)
    got, base = lax.optimization_barrier((turned(z), base))
    far = from_other_core(got)
    full = jnp.stack([side(got, far), side(far, got)], axis=1).reshape(8, 2, 3, half, width)
    y = [half_rows(full[:, :, j].reshape(order, width).T, core) for j in range(3)]
    total = y[2]
    for j in (2, 1):
        total = (dot(total, phis[j]) + y[j - 1].astype(F32)).astype(BF16)
    reduced = (base.astype(F32) + dot(total, phis[0])).astype(BF16)

    start = both_halves(moved(reduced, [(c, (c + 1) % chips) for c in range(chips)]))
    after = both_halves(jnp.where(chip == chips - 1, jnp.zeros_like(reduced), reduced))
    part_high = lax.ppermute(part, "core", [(1, 0)])
    second_k = coupling[1]
    through = side(dot(after, other), dot(after, own)).astype(BF16)
    v = dot(side(part_high, after), second_k).astype(BF16)
    w = dot(through, second_k).astype(BF16)
    got = turned(jnp.concatenate([side(v, through), side(w, v)], axis=0))
    return last_close(
        core,
        got.reshape(8, 2, width, width),
        start,
        part,
        precision_blocks,
        coupling,
        own,
        other,
    )


def solution(mesh):
    grid = Mesh(mesh.devices.reshape(4, 4, 2, 8), ("y", "x", "core", "z"))
    return jax.shard_map(
        shards,
        mesh=grid,
        in_specs=(P(("y", "x", "core"), None, "z"), P(("y", "x", "core"), None, None)),
        out_specs=P(("y", "x", "core"), None, "z"),
        check_vma=False,
    )
```

```python
import jax
import jax.numpy as jnp
from jax import lax
from jax.experimental import pallas as pl
from jax.experimental.pallas import tpu as pltpu
from jax.sharding import Mesh, PartitionSpec as P

BF16 = jnp.bfloat16
F32 = jnp.float32
CHIPS = ("y", "x")
VMEM = 60 * 2**20


def dot(left, right):
    return jnp.dot(left, right, preferred_element_type=F32)


def moved(block, pairs):
    return lax.ppermute(block, CHIPS, pairs)


def from_other_core(block):
    return lax.ppermute(block, "core", [(0, 1), (1, 0)])


def turned(rows):
    slabs = lax.axis_size("z")
    m, n = rows.shape
    rows = lax.optimization_barrier(rows)
    pieces = rows.reshape(m, slabs, n // slabs).swapaxes(0, 1)
    return lax.all_to_all(pieces, "z", 0, 0, tiled=True)


def fetch(source, target, sem, pieces=8):
    rows = target.shape[0] // pieces
    for i in range(pieces):
        part = pl.ds(i * rows, rows)
        pltpu.make_async_copy(source.at[part], target.at[part], sem).start()


def chip_close(core, got, first_p, coupling, own, other):
    _, order, width = first_p.shape
    slabs = order // width

    def kernel(core_ref, got_ref, p_ref, k_ref, own_ref, other_ref, part_ref, kept_ref,
               sent_ref, k, low, k_sem, low_sem):
        fetch(k_ref.at[0], k, k_sem)

        @pl.when(core_ref[0] == 0)
        def _():
            fetch(own_ref, low, low_sem)

        @pl.when(core_ref[0] == 1)
        def _():
            fetch(other_ref, low, low_sem)

        y_a = got_ref[:, 0].reshape(order, width).T
        y_b = got_ref[:, 1].reshape(order, width).T
        p = p_ref[0].T.astype(F32)
        pltpu.make_async_copy(k_ref.at[0], k, k_sem).wait()
        both = jnp.dot(
            jnp.concatenate([y_a, y_b], axis=0), k[...], preferred_element_type=F32
        )
        base = p + both[:width]
        part_ref[...] = base.astype(BF16)
        low_core = core_ref[0] == 0
        left = jnp.where(low_core, y_b.astype(F32), both[width:]).astype(BF16)
        pltpu.make_async_copy(own_ref, low, low_sem).wait()
        total = jnp.where(low_core, base, 0.0) + jnp.dot(
            left, low[...], preferred_element_type=F32
        )
        top, bottom = total[: width // 2], total[width // 2 :]
        kept_ref[...] = jnp.where(low_core, top, bottom)
        sent_ref[...] = jnp.where(low_core, bottom, top)

    whole = pl.BlockSpec(memory_space=pltpu.VMEM)
    hbm = pl.BlockSpec(memory_space=pl.ANY)
    return pl.pallas_call(
        kernel,
        in_specs=[pl.BlockSpec(memory_space=pltpu.SMEM), whole, whole, hbm, hbm, hbm],
        out_specs=[whole, whole, whole],
        out_shape=[
            jax.ShapeDtypeStruct((width, order), BF16),
            jax.ShapeDtypeStruct((width // 2, order), F32),
            jax.ShapeDtypeStruct((width // 2, order), F32),
        ],
        scratch_shapes=[
            pltpu.VMEM((order, order), BF16),
            pltpu.VMEM((order, order), BF16),
            pltpu.SemaphoreType.DMA,
            pltpu.SemaphoreType.DMA,
        ],
        cost_estimate=pl.CostEstimate(
            flops=width * order**2 // 8, bytes_accessed=order * order // 8, transcendentals=0
        ),
        compiler_params=pltpu.CompilerParams(vmem_limit_bytes=VMEM),
    )(core.reshape(1), got, first_p, coupling, own, other)


def last_close(core, got, start, part, precision_blocks, coupling, own, other):
    _, order, width = precision_blocks.shape

    def kernel(core_ref, got_ref, start_ref, part_ref, p_ref, k_ref, own_ref, other_ref, out_ref,
               k, high, k_sem, high_sem):
        low_core = core_ref[0] == 0

        @pl.when(low_core)
        def _():
            fetch(other_ref, high, high_sem)

        @pl.when(jnp.logical_not(low_core))
        def _():
            fetch(own_ref, high, high_sem)

        fetch(k_ref.at[1], k, k_sem)
        y_a = got_ref[:, 0].reshape(order, width).T
        y_b = got_ref[:, 1].reshape(order, width).T
        left = jnp.where(low_core, y_b.astype(F32), y_a.astype(F32)).astype(BF16)
        pltpu.make_async_copy(own_ref, high, high_sem).wait()
        w = jnp.dot(left, high[...], preferred_element_type=F32)
        q = jnp.where(low_core, y_a.astype(F32) + w, y_b.astype(F32)).astype(BF16)
        pltpu.make_async_copy(k_ref.at[1], k, k_sem).wait()
        second = jnp.dot(q, k[...], preferred_element_type=F32)
        out_ref[1] = (p_ref[0].astype(F32) + second.T).astype(BF16)
        first = jnp.where(low_core, start_ref[...].astype(F32), part_ref[...].astype(F32) + w)
        out_ref[0] = first.astype(BF16).T

    whole = pl.BlockSpec(memory_space=pltpu.VMEM)
    hbm = pl.BlockSpec(memory_space=pl.ANY)
    return pl.pallas_call(
        kernel,
        grid=(1,),
        in_specs=[
            pl.BlockSpec(memory_space=pltpu.SMEM),
            whole,
            whole,
            whole,
            pl.BlockSpec((1, order, width), lambda i: (1, 0, 0)),
            hbm,
            hbm,
            hbm,
        ],
        out_specs=pl.BlockSpec((2, order, width), lambda i: (0, 0, 0)),
        out_shape=jax.ShapeDtypeStruct((2, order, width), BF16),
        scratch_shapes=[
            pltpu.VMEM((order, order), BF16),
            pltpu.VMEM((order, order), BF16),
            pltpu.SemaphoreType.DMA,
            pltpu.SemaphoreType.DMA,
        ],
        cost_estimate=pl.CostEstimate(
            flops=4 * width * order**2, bytes_accessed=5 * order * order, transcendentals=0
        ),
        compiler_params=pltpu.CompilerParams(vmem_limit_bytes=VMEM),
    )(core.reshape(1), got, start, part, precision_blocks, coupling, own, other)


def shards(precision_blocks, coupling):
    core = lax.axis_index("core")
    slab = lax.axis_index("z")
    chip = lax.axis_index(CHIPS)
    chips = lax.axis_size(CHIPS)
    order, width = precision_blocks.shape[1:]
    half = width // 2

    def side(a, b):
        return jnp.where(core == 0, a, b)

    def half_rows(block, which):
        return lax.dynamic_slice_in_dim(block, which * half, half, 0)

    def both_halves(block):
        far = from_other_core(block)
        return side(jnp.concatenate([block, far], axis=0), jnp.concatenate([far, block], axis=0))

    def later(distance):
        return [(i + distance, i) for i in range(chips - distance)]

    def ahead_by(distance):
        return [((e + distance), (e - 1) % chips) for e in range(chips - distance)]

    p_high = lax.ppermute(precision_blocks[0], "core", [(1, 0)])
    own = dot(coupling[1], coupling[0]).astype(BF16)
    other = from_other_core(own)
    z_a = lax.dot_general(
        precision_blocks[1], coupling[0], (((0,), (0,)), ((), ())), preferred_element_type=F32
    ).astype(BF16)
    z_b = side(dot(p_high.T, own), dot(z_a, other)).astype(BF16)

    pieces = jnp.concatenate([z_a, z_b], axis=0)
    pieces = pieces.reshape(2 * width, order // width, width).swapaxes(0, 1)
    pieces, other2 = lax.optimization_barrier((pieces, other))
    got = lax.all_to_all(pieces, "z", 0, 0, tiled=True)
    whole = dot(side(other2, own), side(own, other2)).astype(BF16)
    piece = lax.dynamic_slice_in_dim(whole, slab * width + core * half, half, 0)
    piece = dot(moved(piece, later(1)), whole).astype(BF16)
    got, piece = lax.optimization_barrier((got, piece))
    phi2 = lax.all_gather(piece, ("z", "core"), axis=0, tiled=True)
    hop = moved(piece, later(1))

    part, kept, sent = chip_close(
        core, got.reshape(8, 2, width, width), precision_blocks[:1], coupling, own, other
    )
    hop, kept = lax.optimization_barrier((hop, kept))
    piece = dot(hop, whole).astype(BF16)
    piece = dot(moved(piece, later(1)), whole).astype(BF16)
    pieces = [moved(piece, ahead_by(d)) for d in (0, 4, 8)]
    reduced = (kept + from_other_core(sent)).astype(BF16)

    def closed(base, got, times):
        far = from_other_core(got)
        full = jnp.stack([side(got, far), side(far, got)], axis=1).reshape(order, width)
        y = half_rows(full.T, core)
        return (base.astype(F32) + times(y)).astype(BF16)

    times = lambda x: dot(x, whole)
    x = moved(reduced, later(1))
    part_high = lax.ppermute(part, "core", [(1, 0)])
    x, pieces, part_high = lax.optimization_barrier((x, pieces, part_high))
    gathered = lax.all_gather(jnp.stack(pieces), ("z", "core"), axis=1, tiled=True)
    reduced = closed(reduced, turned(times(x).astype(BF16)), times)
    times = lambda x: dot(x, phi2)
    x = moved(reduced, later(2))
    reduced = closed(reduced, turned(times(x).astype(BF16)), times)

    x1, x2, x3 = (moved(reduced, ahead_by(d)) for d in (4, 8, 12))
    base = moved(reduced, ahead_by(0))
    phis = lax.optimization_barrier((gathered[0], gathered[1], gathered[2]))
    z = dot(x3, phis[2]).astype(BF16)
    z = dot(jnp.concatenate([x2, z], axis=0), phis[1]).astype(BF16)
    z = dot(jnp.concatenate([x1, z], axis=0), phis[0]).astype(BF16)
    phi8 = dot(phis[1], phis[0]).astype(BF16)
    phi12 = dot(phis[2], phi8).astype(BF16)
    got, base, phi8, phi12 = lax.optimization_barrier((turned(z), base, phi8, phi12))
    far = from_other_core(got)
    full = jnp.stack([side(got, far), side(far, got)], axis=1).reshape(8, 2, 3, half, width)
    y = [half_rows(full[:, :, j].reshape(order, width).T, core) for j in range(3)]
    total = dot(y[0], phis[0]) + dot(y[1], phi8) + dot(y[2], phi12)
    reduced = (base.astype(F32) + total).astype(BF16)

    start = both_halves(moved(reduced, [(c, (c + 1) % chips) for c in range(chips)]))
    after = both_halves(jnp.where(chip == chips - 1, jnp.zeros_like(reduced), reduced))
    second_k = coupling[1]
    through = side(dot(after, other), dot(after, own)).astype(BF16)
    v = dot(side(part_high, after), second_k).astype(BF16)
    w = dot(through, second_k).astype(BF16)
    got = turned(jnp.concatenate([side(v, through), side(w, v)], axis=0))
    return last_close(
        core,
        got.reshape(8, 2, width, width),
        start,
        part,
        precision_blocks,
        coupling,
        own,
        other,
    )


def solution(mesh):
    grid = Mesh(mesh.devices.reshape(4, 4, 2, 8), ("y", "x", "core", "z"))
    return jax.shard_map(
        shards,
        mesh=grid,
        in_specs=(P(("y", "x", "core"), None, "z"), P(("y", "x", "core"), None, None)),
        out_specs=P(("y", "x", "core"), None, "z"),
        check_vma=False,
    )
```

```python
import jax
import jax.numpy as jnp
from jax import lax
from jax.experimental import pallas as pl
from jax.experimental.pallas import tpu as pltpu
from jax.sharding import Mesh, PartitionSpec as P

BF16 = jnp.bfloat16
F32 = jnp.float32
CHIPS = ("y", "x")
VMEM = 60 * 2**20


def dot(left, right):
    return jnp.dot(left, right, preferred_element_type=F32)


def moved(block, pairs):
    return lax.ppermute(block, CHIPS, pairs)


def from_other_core(block):
    return lax.ppermute(block, "core", [(0, 1), (1, 0)])


def turned(rows):
    slabs = lax.axis_size("z")
    m, n = rows.shape
    rows = lax.optimization_barrier(rows)
    pieces = rows.reshape(m, slabs, n // slabs).swapaxes(0, 1)
    return lax.all_to_all(pieces, "z", 0, 0, tiled=True)


def fetch(source, target, sem, pieces=8):
    rows = target.shape[0] // pieces
    for i in range(pieces):
        part = pl.ds(i * rows, rows)
        pltpu.make_async_copy(source.at[part], target.at[part], sem).start()


def chip_close(core, got, first_p, coupling, own, other):
    _, order, width = first_p.shape
    slabs = order // width

    def kernel(core_ref, got_ref, p_ref, k_ref, own_ref, other_ref, part_ref, kept_ref,
               sent_ref, k, low, k_sem, low_sem):
        fetch(k_ref.at[0], k, k_sem)

        @pl.when(core_ref[0] == 0)
        def _():
            fetch(own_ref, low, low_sem)

        @pl.when(core_ref[0] == 1)
        def _():
            fetch(other_ref, low, low_sem)

        y_a = got_ref[:, 0].reshape(order, width).T
        y_b = got_ref[:, 1].reshape(order, width).T
        p = p_ref[0].T.astype(F32)
        pltpu.make_async_copy(k_ref.at[0], k, k_sem).wait()
        both = jnp.dot(
            jnp.concatenate([y_a, y_b], axis=0), k[...], preferred_element_type=F32
        )
        base = p + both[:width]
        part_ref[...] = base.astype(BF16)
        low_core = core_ref[0] == 0
        left = jnp.where(low_core, y_b.astype(F32), both[width:]).astype(BF16)
        pltpu.make_async_copy(own_ref, low, low_sem).wait()
        total = jnp.where(low_core, base, 0.0) + jnp.dot(
            left, low[...], preferred_element_type=F32
        )
        top, bottom = total[: width // 2], total[width // 2 :]
        kept_ref[...] = jnp.where(low_core, top, bottom)
        sent_ref[...] = jnp.where(low_core, bottom, top)

    whole = pl.BlockSpec(memory_space=pltpu.VMEM)
    hbm = pl.BlockSpec(memory_space=pl.ANY)
    return pl.pallas_call(
        kernel,
        in_specs=[pl.BlockSpec(memory_space=pltpu.SMEM), whole, whole, hbm, hbm, hbm],
        out_specs=[whole, whole, whole],
        out_shape=[
            jax.ShapeDtypeStruct((width, order), BF16),
            jax.ShapeDtypeStruct((width // 2, order), F32),
            jax.ShapeDtypeStruct((width // 2, order), F32),
        ],
        scratch_shapes=[
            pltpu.VMEM((order, order), BF16),
            pltpu.VMEM((order, order), BF16),
            pltpu.SemaphoreType.DMA,
            pltpu.SemaphoreType.DMA,
        ],
        cost_estimate=pl.CostEstimate(
            flops=width * order**2 // 8, bytes_accessed=order * order // 8, transcendentals=0
        ),
        compiler_params=pltpu.CompilerParams(vmem_limit_bytes=VMEM),
    )(core.reshape(1), got, first_p, coupling, own, other)


def last_close(core, got, start, part, precision_blocks, coupling, own, other):
    _, order, width = precision_blocks.shape

    def kernel(core_ref, got_ref, start_ref, part_ref, p_ref, k_ref, own_ref, other_ref, out_ref,
               k, high, k_sem, high_sem):
        low_core = core_ref[0] == 0

        @pl.when(low_core)
        def _():
            fetch(other_ref, high, high_sem)

        @pl.when(jnp.logical_not(low_core))
        def _():
            fetch(own_ref, high, high_sem)

        fetch(k_ref.at[1], k, k_sem)
        y_a = got_ref[:, 0].reshape(order, width).T
        y_b = got_ref[:, 1].reshape(order, width).T
        left = jnp.where(low_core, y_b.astype(F32), y_a.astype(F32)).astype(BF16)
        pltpu.make_async_copy(own_ref, high, high_sem).wait()
        w = jnp.dot(left, high[...], preferred_element_type=F32)
        q = jnp.where(low_core, y_a.astype(F32) + w, y_b.astype(F32)).astype(BF16)
        pltpu.make_async_copy(k_ref.at[1], k, k_sem).wait()
        second = jnp.dot(q, k[...], preferred_element_type=F32)
        out_ref[1] = (p_ref[0].astype(F32) + second.T).astype(BF16)
        first = jnp.where(low_core, start_ref[...].astype(F32), part_ref[...].astype(F32) + w)
        out_ref[0] = first.astype(BF16).T

    whole = pl.BlockSpec(memory_space=pltpu.VMEM)
    hbm = pl.BlockSpec(memory_space=pl.ANY)
    return pl.pallas_call(
        kernel,
        grid=(1,),
        in_specs=[
            pl.BlockSpec(memory_space=pltpu.SMEM),
            whole,
            whole,
            whole,
            pl.BlockSpec((1, order, width), lambda i: (1, 0, 0)),
            hbm,
            hbm,
            hbm,
        ],
        out_specs=pl.BlockSpec((2, order, width), lambda i: (0, 0, 0)),
        out_shape=jax.ShapeDtypeStruct((2, order, width), BF16),
        scratch_shapes=[
            pltpu.VMEM((order, order), BF16),
            pltpu.VMEM((order, order), BF16),
            pltpu.SemaphoreType.DMA,
            pltpu.SemaphoreType.DMA,
        ],
        cost_estimate=pl.CostEstimate(
            flops=4 * width * order**2, bytes_accessed=5 * order * order, transcendentals=0
        ),
        compiler_params=pltpu.CompilerParams(vmem_limit_bytes=VMEM),
    )(core.reshape(1), got, start, part, precision_blocks, coupling, own, other)


def shards(precision_blocks, coupling):
    core = lax.axis_index("core")
    slab = lax.axis_index("z")
    chip = lax.axis_index(CHIPS)
    chips = lax.axis_size(CHIPS)
    order, width = precision_blocks.shape[1:]
    half = width // 2

    def side(a, b):
        return jnp.where(core == 0, a, b)

    def half_rows(block, which):
        return lax.dynamic_slice_in_dim(block, which * half, half, 0)

    def both_halves(block):
        far = from_other_core(block)
        return side(jnp.concatenate([block, far], axis=0), jnp.concatenate([far, block], axis=0))

    def later(distance):
        return [(i + distance, i) for i in range(chips - distance)]

    def ahead_by(distance):
        return [((e + distance), (e - 1) % chips) for e in range(chips - distance)]

    p_high = lax.ppermute(precision_blocks[0], "core", [(1, 0)])
    own = dot(coupling[1], coupling[0]).astype(BF16)
    other = from_other_core(own)
    z_a = lax.dot_general(
        precision_blocks[1], coupling[0], (((0,), (0,)), ((), ())), preferred_element_type=F32
    ).astype(BF16)
    z_b = side(dot(p_high.T, own), dot(z_a, other)).astype(BF16)

    pieces = jnp.concatenate([z_a, z_b], axis=0)
    pieces = pieces.reshape(2 * width, order // width, width).swapaxes(0, 1)
    pieces, other2 = lax.optimization_barrier((pieces, other))
    got = lax.all_to_all(pieces, "z", 0, 0, tiled=True)
    whole = dot(side(other2, own), side(own, other2)).astype(BF16)
    piece = lax.dynamic_slice_in_dim(whole, slab * width + core * half, half, 0)
    piece = dot(moved(piece, later(1)), whole).astype(BF16)
    got, piece = lax.optimization_barrier((got, piece))
    phi2 = lax.all_gather(piece, ("z", "core"), axis=0, tiled=True)
    hop = moved(piece, later(1))

    part, kept, sent = chip_close(
        core, got.reshape(8, 2, width, width), precision_blocks[:1], coupling, own, other
    )
    hop, kept = lax.optimization_barrier((hop, kept))
    piece = dot(hop, whole).astype(BF16)
    piece = dot(moved(piece, later(1)), whole).astype(BF16)
    pieces = [moved(piece, ahead_by(d)) for d in (0, 4, 8)]
    reduced = (kept + from_other_core(sent)).astype(BF16)

    def closed(base, got, times):
        far = from_other_core(got)
        full = jnp.stack([side(got, far), side(far, got)], axis=1).reshape(order, width)
        y = half_rows(full.T, core)
        return (base.astype(F32) + times(y)).astype(BF16)

    times = lambda x: dot(x, whole)
    x = moved(reduced, later(1))
    part_high = lax.ppermute(part, "core", [(1, 0)])
    x, pieces, part_high = lax.optimization_barrier((x, pieces, part_high))
    gathered = lax.all_gather(jnp.stack(pieces), ("z", "core"), axis=1, tiled=True)
    reduced = closed(reduced, turned(times(x).astype(BF16)), times)
    times = lambda x: dot(x, phi2)
    x = moved(reduced, later(2))
    reduced = closed(reduced, turned(times(x).astype(BF16)), times)

    x1, x2, x3 = (moved(reduced, ahead_by(d)) for d in (4, 8, 12))
    base = moved(reduced, ahead_by(0))
    phis = lax.optimization_barrier((gathered[0], gathered[1], gathered[2]))
    z = dot(x3, phis[2]).astype(BF16)
    z = dot(jnp.concatenate([x2, z], axis=0), phis[1]).astype(BF16)
    z = dot(jnp.concatenate([x1, z], axis=0), phis[0]).astype(BF16)
    phi8 = dot(phis[1], phis[0]).astype(BF16)
    phi12 = dot(phis[2], phi8).astype(BF16)
    got, base, phi8, phi12 = lax.optimization_barrier((turned(z), base, phi8, phi12))
    far = from_other_core(got)
    full = jnp.stack([side(got, far), side(far, got)], axis=1).reshape(8, 2, 3, half, width)
    y = [half_rows(full[:, :, j].reshape(order, width).T, core) for j in range(3)]
    total = dot(y[2], phi12) + dot(y[1], phi8)
    total = lax.optimization_barrier(total) + dot(y[0], phis[0])
    reduced = (base.astype(F32) + total).astype(BF16)

    start = both_halves(moved(reduced, [(c, (c + 1) % chips) for c in range(chips)]))
    after = both_halves(jnp.where(chip == chips - 1, jnp.zeros_like(reduced), reduced))
    second_k = coupling[1]
    through = side(dot(after, other), dot(after, own)).astype(BF16)
    v = dot(side(part_high, after), second_k).astype(BF16)
    w = dot(through, second_k).astype(BF16)
    got = turned(jnp.concatenate([side(v, through), side(w, v)], axis=0))
    return last_close(
        core,
        got.reshape(8, 2, width, width),
        start,
        part,
        precision_blocks,
        coupling,
        own,
        other,
    )


def solution(mesh):
    grid = Mesh(mesh.devices.reshape(4, 4, 2, 8), ("y", "x", "core", "z"))
    return jax.shard_map(
        shards,
        mesh=grid,
        in_specs=(P(("y", "x", "core"), None, "z"), P(("y", "x", "core"), None, None)),
        out_specs=P(("y", "x", "core"), None, "z"),
        check_vma=False,
    )
```
